32 devices in a mesh: groups: 2 (over y), gx: 4 (over z), gy: 4 (over x, core).
Axes of the slice: x: 2, y: 2, z: 4, core: 2. Of those that a mesh axis runs over, the one named last changes fastest.
Arguments:
- latent: bfloat16 [32, 32, 8, 256], P(('groups', 'gx'), 'gy'), parts along dimension 0, may hold values from -6 to 6
- positions: bfloat16 [32, 32, 8, 2], P(('groups', 'gx'), 'gy'), parts along dimension 0, may hold values from 0 to 1
- counts: int32 [32, 32], P(('groups', 'gx'), 'gy'), parts along dimension 0, may hold values from 1 to 8, as said below
- cotangent: bfloat16 [32, 32, 8, 256], P(('groups', 'gx'), 'gy'), parts along dimension 0, may hold values from -6 to 6
- w_recv: bfloat16 [256, 256], replicated, may hold values from -0.375 to 0.375
- w_send: bfloat16 [256, 256], replicated, may hold values from -0.375 to 0.375
- w_msg: bfloat16 [256, 256], replicated, may hold values from -0.375 to 0.375
- w_node_h: bfloat16 [256, 256], replicated, may hold values from -0.375 to 0.375
- w_node_m: bfloat16 [256, 256], replicated, may hold values from -0.375 to 0.375
- w_out: bfloat16 [256, 256], replicated, may hold values from -0.375 to 0.375
- geometry: float32 [3, 256], replicated, may hold values from -3 to 3
- gain: float32 [256], replicated, may hold values from 0.5 to 1.5
Outputs:
- latent_out: bfloat16 [32, 32, 8, 256], P(('groups', 'gx'), 'gy'), parts along dimension 0
- grad_latent: bfloat16 [32, 32, 8, 256], P(('groups', 'gx'), 'gy'), parts along dimension 0
- grad_recv: float32 [512, 256], P('groups'), parts along dimension 0
- grad_send: float32 [512, 256], P('groups'), parts along dimension 0
- grad_msg: float32 [512, 256], P('groups'), parts along dimension 0
- grad_node_h: float32 [512, 256], P('groups'), parts along dimension 0
- grad_node_m: float32 [512, 256], P('groups'), parts along dimension 0
- grad_out: float32 [512, 256], P('groups'), parts along dimension 0
- grad_geometry: float32 [6, 256], P('groups'), parts along dimension 0
- grad_gain: float32 [512], P('groups'), parts along dimension 0
The draws below stay inside these ranges and needn't reach their ends.
There are 2 independent parts, one for each index of `groups`. The reference program is written for one: setup_inputs(seed, part) draws one part's arguments, and reference() takes and returns one part's arrays. A program takes and returns all parts, laid end to end along the dimension named above; an argument that names none is the same for every part. Nothing has to cross between parts.
Inputs may be any that keep to these rules, and one draw needn't show every extreme that they name: `counts`: slots below a cell's count hold particles, the others are padding; some cell holds 8 particles in every draw, and whole blocks of 4 x 8 cells are one to four times denser than others.
All inputs are finite; a program needn't handle non-finite values.
Results may differ from the reference program's by a relative error of at most 0.019.
The reference program's roundings to bfloat16 on the way (of `send_proj`, `aggregate`, `message` and `active`) count: a program that leaves them out, or rounds other values in their place, can miss the bound.
Values may be sent and summed in bfloat16 or wider, within the bound.
A program may use at most 64 MiB of HBM per device.

```python
from functools import partial
import jax
import jax.numpy as jnp
from jax import lax

W = 256
S = 8
STEPS = 2
CX = 4
CY = 8
NX = 16
NY = 32


def draw_counts(key, part):
    key = jax.random.fold_in(key, 11)
    key_base, key_dense, key_x, key_y = jax.random.split(key, 4)
    baseline = jax.random.randint(key_base, (NX, NY), 1, S // 2 + 1)
    density = jax.random.randint(key_dense, (NX // CX, NY // CY), 1, 5)
    density = jnp.repeat(jnp.repeat(density, CX, axis=0), CY, axis=1)
    filled = jnp.minimum(baseline * density, S)
    full_x = jax.random.randint(key_x, (), 0, NX)
    full_y = jax.random.randint(key_y, (), 0, NY)
    filled = filled.at[full_x, full_y].set(S)
    return filled.astype(jnp.int32)


def block_scale(stream_key, shape, cuts, low, top_value):
    level = 1.0
    for axis_at, blocks in cuts:
        steps = jax.random.uniform(jax.random.fold_in(jax.random.fold_in(stream_key, 6), axis_at), (blocks,), jnp.float32, low / len(cuts), top_value / len(cuts))
        level = level * jnp.repeat(jnp.exp(steps), shape[axis_at] // blocks).reshape((-1,) + (1,) * (len(shape) - 1 - axis_at))
    return level


def gaussian(rng, extent, scale, limit, cuts=(), held_as=jnp.bfloat16):
    level = block_scale(rng, extent, cuts, -0.22, 0.18) if cuts else 1.0
    result = jax.random.normal(rng, extent, jnp.float32) * scale * level
    return jnp.minimum(jnp.maximum(result, -limit), limit).astype(held_as)


def setup_inputs(seed: int = 0, part: int = 0) -> dict:
    splits = jax.random.split(jax.random.key(seed), 13)
    own_keys = jax.random.split(jax.random.fold_in(splits[12], part), 13)
    return {
        "latent": gaussian(own_keys[0], (NX, NY, S, W), 1.0, 6.0, ((0, 4), (1, 4))),
        "positions": jnp.clip(1.0 * jax.random.uniform(own_keys[1], (NX, NY, S, 2), jnp.float32) ** block_scale(own_keys[1], (NX, NY, S, 2), ((0, 4), (1, 4)), -0.2, 0.2), 0.0, 1.0).astype(jnp.bfloat16),
        "counts": draw_counts(jax.random.fold_in(jax.random.fold_in(splits[12], part), 71), part),
        "cotangent": gaussian(own_keys[3], (NX, NY, S, W), 1.0, 6.0, ((0, 4), (1, 4))),
        "w_recv": gaussian(splits[4], (W, W), W ** -0.5, 0.375),
        "w_send": gaussian(splits[5], (W, W), W ** -0.5, 0.375),
        "w_msg": gaussian(splits[6], (W, W), W ** -0.5, 0.375),
        "w_node_h": gaussian(splits[7], (W, W), W ** -0.5, 0.375),
        "w_node_m": gaussian(splits[8], (W, W), W ** -0.5, 0.375),
        "w_out": gaussian(splits[9], (W, W), W ** -0.5, 0.375),
        "geometry": gaussian(splits[10], (3, W), 0.5, 3.0, (), jnp.float32),
        "gain": jnp.clip(1.0 + 0.1 * jax.random.normal(splits[11], (W,), jnp.float32), 0.5, 1.5),
    }


EPSILON = 1e-05
OFFSETS = ((-1, -1), (-1, 0), (-1, 1), (0, -1), (0, 0), (0, 1), (1, -1), (1, 0), (1, 1))

def pair_row(shift_x, shift_y, geometry, pieces):
    recv_proj, send_proj, recv_pos, send_pos, recv_valid, send_valid = pieces
    disp_x = send_pos[..., None, :, 0] + shift_x - recv_pos[..., :, None, 0]
    disp_y = send_pos[..., None, :, 1] + shift_y - recv_pos[..., :, None, 1]
    dist_sq = disp_x * disp_x + disp_y * disp_y
    pair_weight = recv_valid[..., :, None] * send_valid[..., None, :] / (1.0 + dist_sq)
    if shift_x == 0 and shift_y == 0:
        slots = recv_proj.shape[-2]
        pair_weight = pair_weight * (1.0 - jnp.eye(slots, dtype=jnp.float32))
    preact = recv_proj[..., :, None, :] + send_proj[..., None, :, :] + disp_x[..., None] * geometry[0] + disp_y[..., None] * geometry[1] + dist_sq[..., None] * geometry[2]
    return lax.optimization_barrier(jnp.sum(pair_weight[..., None] * jax.nn.silu(preact), axis=-2))

def offset_terms(shift_x, shift_y, geometry, pieces):
    row_fn = jax.checkpoint(partial(pair_row, shift_x, shift_y, geometry))
    return lax.map(row_fn, pieces)

def layer_norm(values, gain):
    center = values - lax.optimization_barrier(jnp.mean(values, axis=-1, keepdims=True))
    spread = lax.optimization_barrier(jnp.mean(center * center, axis=-1, keepdims=True))
    return center * lax.rsqrt(spread + EPSILON) * gain

def send_part(w_send, latent32, tap_send):
    product = jnp.dot(latent32.astype(jnp.bfloat16), w_send, preferred_element_type=jnp.float32)
    return (product + tap_send).astype(jnp.bfloat16)

def receive_part(weights, positions32, validity, latent32, send32, tap_recv, tap_msg, tap_pre, tap_out, geometry, gain):
    w_recv, w_msg, w_node_h, w_node_m, w_out = weights
    latent16 = latent32.astype(jnp.bfloat16)
    recv_proj = jnp.dot(latent16, w_recv, preferred_element_type=jnp.float32) + tap_recv
    total = jnp.zeros(recv_proj.shape, jnp.float32)
    for shift_x, shift_y in OFFSETS:
        send_proj = jnp.roll(send32, (-shift_x, -shift_y), (0, 1))
        send_pos = jnp.roll(positions32, (-shift_x, -shift_y), (0, 1))
        send_valid = jnp.roll(validity, (-shift_x, -shift_y), (0, 1))
        total = total + offset_terms(shift_x, shift_y, geometry, (recv_proj, send_proj, positions32, send_pos, validity, send_valid))
    aggregate = total.astype(jnp.bfloat16)
    message = (jnp.dot(aggregate, w_msg, preferred_element_type=jnp.float32) + tap_msg).astype(jnp.bfloat16)
    hidden = jnp.dot(latent16, w_node_h, preferred_element_type=jnp.float32) + jnp.dot(message, w_node_m, preferred_element_type=jnp.float32) + tap_pre
    active = jax.nn.silu(hidden).astype(jnp.bfloat16)
    output = jnp.dot(active, w_out, preferred_element_type=jnp.float32) + tap_out
    updated = (latent32 + layer_norm(output, gain)).astype(jnp.bfloat16)
    return (updated, (latent16, aggregate, message, active))

def outer_sum(inputs16, derivs):
    width = derivs.shape[-1]
    return lax.dot_general(inputs16.reshape(-1, inputs16.shape[-1]).astype(jnp.float32), derivs.reshape(-1, width), (((0,), (0,)), ((), ())), precision=lax.Precision.HIGHEST)

def reference(latent, positions, counts, cotangent, w_recv, w_send, w_msg, w_node_h, w_node_m, w_out, geometry, gain):
    positions32 = positions.astype(jnp.float32)
    slot_index = jnp.arange(counts.shape[0] * 0 + latent.shape[2], dtype=jnp.int32)
    validity = (slot_index[None, None, :] < counts[:, :, None]).astype(jnp.float32)
    weights = (w_recv, w_msg, w_node_h, w_node_m, w_out)
    zeros = jnp.zeros(latent.shape, jnp.float32)
    records = []
    current = latent
    for step in range(STEPS):
        latent32 = current.astype(jnp.float32)
        send16, send_back = jax.vjp(partial(send_part, w_send), latent32, zeros)
        updated, recv_back, saved = jax.vjp(partial(receive_part, weights, positions32, validity), latent32, send16.astype(jnp.float32), zeros, zeros, zeros, zeros, geometry, gain, has_aux=True)
        records.append((send_back, recv_back, saved))
        current = updated
    latent_out = current
    flow = cotangent
    grads = [jnp.zeros((latent.shape[3], latent.shape[3]), jnp.float32) for index in range(6)]
    grad_geometry = jnp.zeros(geometry.shape, jnp.float32)
    grad_gain = jnp.zeros(gain.shape, jnp.float32)
    for send_back, recv_back, saved in reversed(records):
        g_latent, g_send32, g_recv, g_msg, g_pre, g_out, g_geom, g_gain = recv_back(flow)
        g_latent_b, g_tap_send = send_back(g_send32.astype(jnp.bfloat16))
        latent16, aggregate, message, active = saved
        grads[0] = grads[0] + outer_sum(latent16, g_recv)
        grads[1] = grads[1] + outer_sum(latent16, g_tap_send)
        grads[2] = grads[2] + outer_sum(aggregate, g_msg)
        grads[3] = grads[3] + outer_sum(latent16, g_pre)
        grads[4] = grads[4] + outer_sum(message, g_pre)
        grads[5] = grads[5] + outer_sum(active, g_out)
        grad_geometry = grad_geometry + g_geom
        grad_gain = grad_gain + g_gain
        flow = (g_latent + g_latent_b).astype(jnp.bfloat16)
    return (latent_out, flow, grads[0], grads[1], grads[2], grads[3], grads[4], grads[5], grad_geometry, grad_gain)
```

```python
from functools import partial

import jax
import jax.numpy as jnp
from jax import lax
from jax.experimental import pallas as pl
from jax.experimental.pallas import tpu as pltpu
from jax.sharding import PartitionSpec as P

STEPS = 2
EPSILON = 1e-05
OFFSETS = ((-1, -1), (-1, 0), (-1, 1), (0, -1), (0, 0), (0, 1), (1, -1), (1, 0), (1, 1))
SIDES = ((1, 0), (-1, 0), (0, 1), (0, -1), (1, 1), (1, -1), (-1, 1), (-1, -1))
MESH = pl.DeviceIdType.MESH
F32 = jnp.float32
BF16 = jnp.bfloat16
SEND_AT = 16
GEO_AT = 88
DEPTH = 128


def round16(rows):
    return -(-rows // 16) * 16


def mm(a, b):
    return jnp.dot(a.astype(BF16), b.astype(BF16), preferred_element_type=F32)


def mm_t(a, b):
    return lax.dot_general(
        a.astype(BF16), b.astype(BF16), (((1,), (1,)), ((), ())), preferred_element_type=F32
    )


def outer(a, b):
    return lax.dot_general(
        a.astype(BF16), b.astype(BF16), (((0,), (0,)), ((), ())), preferred_element_type=F32
    )


def rounded(value):
    return value.astype(BF16).astype(F32)


def segments(cx, cy, slots):
    found, at = [], 0
    for dx, dy in SIDES:
        rows = round16((cx if dx == 0 else 1) * (cy if dy == 0 else 1) * slots)
        found.append((at, rows))
        at += rows
    return found, at


def span(step, size, low, high):
    if step == 0:
        return range(1, size + 1)
    return [high] if step == 1 else [low]


def kernel(
    ngx,
    ngy,
    cells_x,
    cells_y,
    h_ref,
    cell_ref,
    cot_ref,
    w_recv,
    w_send,
    w_msg,
    w_nh,
    w_nm,
    w_out,
    geom_ref,
    gain_ref,
    latent_out,
    grad_latent,
    out_a,
    out_b,
    ext,
    gext,
    recv,
    agg,
    g_agg,
    g_recv,
    hs,
    agg16,
    msg16,
    act16,
    hidden,
    xhat,
    rstd,
    acc,
    acc_small,
    acc_geo,
    pos_send,
    pos_recv,
    pos_ext,
    feat,
    geo,
    mat,
    mat_t,
    weight,
    geo_b,
    halo_send,
    halo_recv,
    part_a,
    part_b,
    got_a,
    got_b,
    pos_sems,
    halo_sems,
    red_sems,
):
    slots = 8
    cells = cells_x * cells_y
    pairs = 9 * slots * slots
    wide = geo.shape[-1]
    n = ngx * ngy
    gx, gy = lax.axis_index("gx"), lax.axis_index("gy")
    me = gx * ngy + gy
    width = h_ref.shape[1]
    segs, _ = segments(cells_x, cells_y, slots)

    def place(dx, dy):
        return {"gx": lax.rem(gx + dx + ngx, ngx), "gy": lax.rem(gy + dy + ngy, ngy)}

    def peer(k):
        other = lax.rem(me + k, n)
        return other, {"gx": lax.div(other, ngy), "gy": lax.rem(other, ngy)}

    barrier = pltpu.get_barrier_semaphore()

    def greet(k, carry):
        _, device = peer(k)
        pl.semaphore_signal(barrier, inc=1, device_id=device, device_id_type=MESH)
        return carry

    lax.fori_loop(1, n, greet, 0)

    def wait_all(ref, sem):
        pltpu.make_async_copy(ref, ref, sem).wait()

    by_cell = cell_ref[...]
    for d, (dx, dy) in enumerate(SIDES):
        xs = [x - 1 for x in span(dx, cells_x, 1, cells_x)]
        if dx != 0 and dy == 0:
            pos_send[d] = by_cell[xs[0]]
        else:
            y = 0 if dy == -1 else cells_y - 1
            rows = [by_cell[x, y : y + 1] for x in xs]
            rows += [rows[-1]] * (cells_y - len(rows))
            pos_send[d] = jnp.concatenate(rows, axis=0)

    h0 = h_ref[...]
    pl.semaphore_wait(barrier, n - 1)
    for d, (dx, dy) in enumerate(SIDES):
        pltpu.make_async_remote_copy(
            pos_send.at[d], pos_recv.at[d], pos_sems.at[0], pos_sems.at[1],
            device_id=place(dx, dy), device_id_type=MESH,
        ).start()

    def start_halo(phase, taken):
        for d, (dx, dy) in enumerate(SIDES):
            at, rows = segs[d]
            tiles = taken(dx, dy)
            tiles = tiles + [tiles[-1]] * (rows // slots - len(tiles))
            halo_send[phase, pl.ds(at, rows)] = jnp.concatenate(tiles, axis=0).astype(BF16)
            pltpu.make_async_remote_copy(
                halo_send.at[phase, pl.ds(at, rows)],
                halo_recv.at[phase, pl.ds(at, rows)],
                halo_sems.at[0, phase],
                halo_sems.at[1, phase],
                device_id=place(dx, dy),
                device_id_type=MESH,
            ).start()

    def end_halo(phase):
        wait_all(halo_recv.at[phase], halo_sems.at[1, phase])
        wait_all(halo_send.at[phase], halo_sems.at[0, phase])

    def project(step, h):
        hs[step] = h
        recv[step] = mm(h, w_recv[...]).reshape(cells, slots, width)
        half = (rounded(mm(h, w_send[...])) * 0.5).reshape(cells_x, cells_y, slots, width)

        def taken(dx, dy):
            return [
                half[x - 1, y - 1]
                for x in span(dx, cells_x, 1, cells_x)
                for y in span(dy, cells_y, 1, cells_y)
            ]

        start_halo(step, taken)
        for x in range(cells_x):
            ext[step, x + 1, pl.ds(1, cells_y)] = half[x]

    def arrive(step):
        end_halo(step)
        for d, (dx, dy) in enumerate(SIDES):
            at, rows = segs[d]
            block = halo_recv[step, pl.ds(at, rows)].astype(F32)
            where = [
                (x, y)
                for x in span(dx, cells_x, cells_x + 1, 0)
                for y in span(dy, cells_y, cells_y + 1, 0)
            ]
            for t, (x, y) in enumerate(where):
                ext[step, x, y] = block[t * slots : (t + 1) * slots]

    project(0, h0)

    g = geom_ref[...] * 0.5
    g_hi = rounded(g)
    g_lo = g - g_hi
    rows = []
    for f in range(3):
        rows += [g_hi[f : f + 1], g_hi[f : f + 1], g_lo[f : f + 1]]
    rows.append(jnp.zeros((DEPTH - GEO_AT - 9, width), F32))
    geo_b[...] = jnp.concatenate(rows, axis=0)

    k_at = lax.broadcasted_iota(jnp.int32, (DEPTH, wide), 0)
    r_at = lax.broadcasted_iota(jnp.int32, (DEPTH, wide), 1)
    takes_recv = (k_at < SEND_AT) & ((r_at & 7) == (k_at & 7))
    takes_send = (k_at >= SEND_AT) & (k_at < GEO_AT) & ((r_at >> 3) == k_at - SEND_AT)
    one_hot = jnp.where((r_at < pairs) & (takes_recv | takes_send), 1.0, 0.0).astype(F32)
    lane = lax.broadcasted_iota(jnp.int32, (1, wide), 1)
    cell_o = lane >> 6
    third = (cell_o >= 3).astype(jnp.int32) + (cell_o >= 6).astype(jnp.int32)
    off_x = (third - 1).astype(F32)
    off_y = (cell_o - third * 3 - 1).astype(F32)
    same = (cell_o == 4) & (((lane >> 3) & 7) == (lane & 7))

    wait_all(pos_recv, pos_sems.at[1])
    wait_all(pos_send, pos_sems.at[0])
    for x in range(cells_x):
        pos_ext[x + 1, pl.ds(1, cells_y)] = by_cell[x]
    for d, (dx, dy) in enumerate(SIDES):
        tile = pos_recv[d]
        xs = list(span(dx, cells_x, cells_x + 1, 0))
        if dx != 0 and dy == 0:
            pos_ext[xs[0], pl.ds(1, cells_y)] = tile
        else:
            y = 0 if dy == 1 else cells_y + 1
            for t, x in enumerate(xs):
                pos_ext[x, pl.ds(y, 1)] = tile[t : t + 1]
    feat[...] = jnp.zeros(feat.shape, F32)
    for x in range(cells_x):
        rows_x = pl.ds(x * cells_y, cells_y)
        for f in range(3):
            own = by_cell[x][:, f * slots : (f + 1) * slots]
            feat[f, rows_x, 0:slots] = own if f == 2 else -own
        for o, (ox, oy) in enumerate(OFFSETS):
            near = pos_ext[x + 1 + ox, pl.ds(1 + oy, cells_y)]
            at = SEND_AT + o * slots
            for f in range(3):
                feat[f, rows_x, at : at + slots] = near[:, f * slots : (f + 1) * slots]
    disp_x = mm(feat[0], one_hot) + off_x
    disp_y = mm(feat[1], one_hot) + off_y
    both = mm(feat[2], one_hot)
    dist = disp_x * disp_x + disp_y * disp_y
    wgt = jnp.where((both > 1.5) & jnp.logical_not(same), 1.0 / (1.0 + dist), 0.0)
    for f, value in enumerate((disp_x, disp_y, dist, wgt)):
        geo[f] = value
    spread_row = lax.broadcasted_iota(jnp.int32, (DEPTH, 128), 0)
    spreads = ((spread_row == GEO_AT + 9) | (spread_row == GEO_AT + 10)).astype(F32).astype(BF16)
    row16 = lax.broadcasted_iota(jnp.int32, (16, wide), 0)

    def prepare(c, carry):
        tile = jnp.zeros((16, wide), F32)
        for f in range(4):
            value = geo[f, pl.ds(c, 1)]
            hi = rounded(value)
            lo = value - hi
            at = 3 * f
            if f < 3:
                tile = jnp.where((row16 == at) | (row16 == at + 2), hi, tile)
            else:
                tile = jnp.where(row16 == at, hi, tile)
            tile = jnp.where(row16 == at + 1, lo, tile)
        full = jnp.concatenate(
            [one_hot[:GEO_AT], tile, jnp.zeros((DEPTH - GEO_AT - 16, wide), F32)], axis=0
        )
        mat_t[c] = full[:, :pairs].astype(BF16)
        turned = full.T[:pairs].astype(BF16)
        mat[c] = turned
        weight[c] = jnp.dot(turned, spreads, preferred_element_type=F32)
        return carry

    lax.fori_loop(0, cells, prepare, 0)

    def half_preact(step, c):
        x, y = lax.div(c, cells_y), lax.rem(c, cells_y)
        r = recv[step, c] * 0.5
        hi = rounded(r)
        tiles = [hi, r - hi]
        tiles += [ext[step, x + 1 + ox, y + 1 + oy] for ox, oy in OFFSETS]
        b = jnp.concatenate(tiles + [geo_b[...]], axis=0).astype(BF16)
        return jnp.dot(mat[c], b, preferred_element_type=F32)

    block = slots * slots

    def weights_of(c, o):
        w = weight[c, o * block : (o + 1) * block]
        return jnp.concatenate([w] * (width // 128), axis=1).reshape(slots, slots, width)

    def forward_pairs(step):
        def body(c, carry):
            q = half_preact(step, c)
            total = jnp.zeros((slots, width), F32)
            for o in range(9):
                part = q[o * block : (o + 1) * block].reshape(slots, slots, width)
                total = total + jnp.sum(weights_of(c, o) * (part + part * jnp.tanh(part)), axis=0)
            agg[c] = total
            return carry

        lax.fori_loop(0, cells, body, 0)

    def backward_pairs(step):
        gext[...] = jnp.zeros(gext.shape, F32)

        def body(c, carry):
            x, y = lax.div(c, cells_y), lax.rem(c, cells_y)
            q = half_preact(step, c)
            up = (g_agg[c] * 0.5)[None]
            parts = []
            for o in range(9):
                part = q[o * block : (o + 1) * block].reshape(slots, slots, width)
                t = jnp.tanh(part)
                d = (weights_of(c, o) * up) * ((1.0 + t) * (1.0 + (part - part * t)))
                parts.append(d.reshape(block, width).astype(BF16))
            back = jnp.dot(mat_t[c], jnp.concatenate(parts, axis=0), preferred_element_type=F32)
            g_recv[c] = back[:slots]
            for o, (ox, oy) in enumerate(OFFSETS):
                at = SEND_AT + o * slots
                gext[x + 1 + ox, y + 1 + oy] += back[at : at + slots]
            acc_geo[...] += back[GEO_AT : GEO_AT + 16]
            return carry

        lax.fori_loop(0, cells, body, 0)

    gain = gain_ref[...]

    def node_forward(step):
        a16 = agg[...].reshape(cells * slots, width).astype(BF16)
        agg16[step] = a16
        m16 = mm(a16, w_msg[...]).astype(BF16)
        msg16[step] = m16
        hid = mm(hs[step], w_nh[...]) + mm(m16, w_nm[...])
        hidden[step] = hid
        half = hid * 0.5
        a = (half + half * jnp.tanh(half)).astype(BF16)
        act16[step] = a
        out = mm(a, w_out[...])
        center = out - jnp.mean(out, axis=-1, keepdims=True)
        scale = lax.rsqrt(jnp.mean(center * center, axis=-1, keepdims=True) + EPSILON)
        normed = center * scale
        xhat[step] = normed
        rstd[step] = jnp.broadcast_to(scale, rstd.shape[1:])
        return (hs[step].astype(F32) + normed * gain).astype(BF16)

    arrive(0)
    forward_pairs(0)
    project(1, node_forward(0))
    arrive(1)
    forward_pairs(1)
    latent_out[...] = node_forward(1)

    def spread_out(part, got, share, sem):
        def one(k, carry):
            other, device = peer(k)
            pltpu.make_async_remote_copy(
                part.at[pl.ds(pl.multiple_of(other * share, 16), share)],
                got.at[k - 1],
                red_sems.at[0, sem],
                red_sems.at[1, sem],
                device_id=device,
                device_id_type=MESH,
            ).start()
            return carry

        lax.fori_loop(1, n, one, 0)

    def gather_in(part, got, share, result, sem):
        wait_all(got, red_sems.at[1, sem])
        wait_all(got, red_sems.at[0, sem])
        mine = pl.ds(pl.multiple_of(me * share, 16), share)
        total = lax.fori_loop(
            0, n - 1, lambda k, t: t + got[k].astype(F32), part[mine].astype(F32)
        )
        result[mine] = total.astype(BF16)

        def one(k, carry):
            _, device = peer(k)
            pltpu.make_async_remote_copy(
                result.at[mine], result.at[mine], red_sems.at[0, sem + 1],
                red_sems.at[1, sem + 1], device_id=device, device_id_type=MESH,
            ).start()
            return carry

        lax.fori_loop(1, n, one, 0)

    def gathered(share, result, sem):
        size = result.at[pl.ds(0, (n - 1) * share)]
        wait_all(size, red_sems.at[1, sem + 1])
        wait_all(size, red_sems.at[0, sem + 1])

    share_a = got_a.shape[1]
    share_b = got_b.shape[1]

    flow = cot_ref[...]
    acc_geo[...] = jnp.zeros(acc_geo.shape, F32)
    for step in (1, 0):
        last = step == 0

        def put(index, term):
            if not last:
                acc[index] = term
                return
            term = (acc[index] + term).astype(BF16)
            if index < 4:
                part_a[pl.ds(index * width, width)] = term
            else:
                part_b[pl.ds((index - 4) * width, width)] = term

        flow32 = flow.astype(F32)
        normed = xhat[step]
        g_gain = jnp.sum(flow32 * normed, axis=0, keepdims=True)
        if last:
            g_gain = g_gain + acc_small[0:1]
        acc_small[...] = jnp.broadcast_to(g_gain, acc_small.shape)
        scaled = flow32 * gain
        d_out = rstd[step][:, :1] * (
            scaled
            - jnp.mean(scaled, axis=-1, keepdims=True)
            - normed * jnp.mean(scaled * normed, axis=-1, keepdims=True)
        )
        put(3, outer(act16[step], d_out))
        d_act = rounded(mm_t(d_out, w_out[...]))
        half = hidden[step] * 0.5
        t = jnp.tanh(half)
        d_hid = (d_act * 0.5) * ((1.0 + t) * (1.0 + (half - half * t)))
        put(1, outer(hs[step], d_hid))
        put(2, outer(msg16[step], d_hid))
        d_msg = mm_t(d_hid, w_nm[...]).astype(BF16)
        put(0, outer(agg16[step], d_msg))
        if last:
            if part_a.shape[0] > 4 * width:
                part_a[pl.ds(4 * width, part_a.shape[0] - 4 * width)] = jnp.zeros(
                    (part_a.shape[0] - 4 * width, width), BF16
                )
            spread_out(part_a, got_a, share_a, 0)
        g_agg[...] = rounded(mm_t(d_msg, w_msg[...])).reshape(cells, slots, width)
        backward_pairs(step)

        def taken(dx, dy):
            return [
                gext[x, y]
                for x in span(dx, cells_x, 0, cells_x + 1)
                for y in span(dy, cells_y, 0, cells_y + 1)
            ]

        start_halo(STEPS + step, taken)
        d_recv = g_recv[...].reshape(cells * slots, width)
        put(4, outer(hs[step], d_recv))
        d_h = flow32 + rounded(mm_t(d_hid, w_nh[...])) + rounded(mm_t(d_recv, w_recv[...]))
        if last:
            gather_in(part_a, got_a, share_a, out_a, 0)
        end_halo(STEPS + step)
        for d, (dx, dy) in enumerate(SIDES):
            at, rows_d = segs[d]
            arrived = halo_recv[STEPS + step, pl.ds(at, rows_d)].astype(F32)
            where = [
                (x, y)
                for x in span(dx, cells_x, cells_x, 1)
                for y in span(dy, cells_y, cells_y, 1)
            ]
            for i, (x, y) in enumerate(where):
                gext[x, y] += arrived[i * slots : (i + 1) * slots]
        d_send = jnp.concatenate(
            [
                gext[x + 1, pl.ds(1, cells_y)].reshape(cells_y * slots, width)
                for x in range(cells_x)
            ],
            axis=0,
        ).astype(BF16)
        put(5, outer(hs[step], d_send))
        if last:
            sums = acc_geo[...]
            tail = [sums[3 * f : 3 * f + 1] + sums[3 * f + 1 : 3 * f + 2] for f in range(3)]
            tail.append(acc_small[0:1])
            rest = part_b.shape[0] - 2 * width
            tail.append(jnp.zeros((rest - 4, width), F32))
            part_b[pl.ds(2 * width, rest)] = jnp.concatenate(tail, axis=0).astype(BF16)
            spread_out(part_b, got_b, share_b, 2)
        flow = (d_h + rounded(mm_t(d_send, w_send[...]))).astype(BF16)
    grad_latent[...] = flow
    gather_in(part_b, got_b, share_b, out_b, 2)
    gathered(share_a, out_a, 0)
    gathered(share_b, out_b, 2)


def per_device(
    ngx,
    ngy,
    latent,
    positions,
    counts,
    cotangent,
    w_recv,
    w_send,
    w_msg,
    w_node_h,
    w_node_m,
    w_out,
    geometry,
    gain,
):
    cells_x, cells_y, slots, width = latent.shape
    cells = cells_x * cells_y
    rows = cells * slots
    n = ngx * ngy
    slot_index = lax.broadcasted_iota(jnp.int32, (cells_x, cells_y, slots), 2)
    validity = (slot_index < counts[:, :, None]).astype(F32)
    by_cell = jnp.concatenate(
        [
            positions[..., 0].astype(F32),
            positions[..., 1].astype(F32),
            validity,
            jnp.zeros((cells_x, cells_y, 128 - 3 * slots), F32),
        ],
        axis=-1,
    )
    pairs = 9 * slots * slots
    wide = -(-pairs // 128) * 128
    _, halo_rows = segments(cells_x, cells_y, slots)
    share_a = round16(-(-4 * width // n))
    share_b = round16(-(-(2 * width + 16) // n))
    vmem = pltpu.VMEM
    scratch = [
        vmem((STEPS, cells_x + 2, cells_y + 2, slots, width), F32),
        vmem((cells_x + 2, cells_y + 2, slots, width), F32),
        vmem((STEPS, cells, slots, width), F32),
        vmem((cells, slots, width), F32),
        vmem((cells, slots, width), F32),
        vmem((cells, slots, width), F32),
        vmem((STEPS, rows, width), BF16),
        vmem((STEPS, rows, width), BF16),
        vmem((STEPS, rows, width), BF16),
        vmem((STEPS, rows, width), BF16),
        vmem((STEPS, rows, width), F32),
        vmem((STEPS, rows, width), F32),
        vmem((STEPS, rows, 128), F32),
        vmem((6, width, width), F32),
        vmem((8, width), F32),
        vmem((16, width), F32),
        vmem((8, cells_y, 128), F32),
        vmem((8, cells_y, 128), F32),
        vmem((cells_x + 2, -(-(cells_y + 2) // 8) * 8, 128), F32),
        vmem((3, cells, 128), F32),
        vmem((4, cells, wide), F32),
        vmem((cells, pairs, DEPTH), BF16),
        vmem((cells, DEPTH, pairs), BF16),
        vmem((cells, pairs, 128), F32),
        vmem((DEPTH - GEO_AT, width), F32),
        vmem((2 * STEPS, halo_rows, width), BF16),
        vmem((2 * STEPS, halo_rows, width), BF16),
        vmem((n * share_a, width), BF16),
        vmem((n * share_b, width), BF16),
        vmem((n - 1, share_a, width), BF16),
        vmem((n - 1, share_b, width), BF16),
        pltpu.SemaphoreType.DMA((2,)),
        pltpu.SemaphoreType.DMA((2, 2 * STEPS)),
        pltpu.SemaphoreType.DMA((2, 4)),
    ]
    spec = pl.BlockSpec(memory_space=pltpu.VMEM)
    new, flow, sums_a, sums_b = pl.pallas_call(
        partial(kernel, ngx, ngy, cells_x, cells_y),
        out_shape=[
            jax.ShapeDtypeStruct((rows, width), BF16),
            jax.ShapeDtypeStruct((rows, width), BF16),
            jax.ShapeDtypeStruct((n * share_a, width), BF16),
            jax.ShapeDtypeStruct((n * share_b, width), BF16),
        ],
        in_specs=[spec] * 11,
        out_specs=[spec] * 4,
        scratch_shapes=scratch,
        compiler_params=pltpu.CompilerParams(
            collective_id=0, has_side_effects=True, vmem_limit_bytes=56 * 2**20
        ),
        name="evolver",
    )(
        latent.reshape(rows, width),
        by_cell,
        cotangent.reshape(rows, width),
        w_recv,
        w_send,
        w_msg,
        w_node_h,
        w_node_m,
        w_out,
        geometry,
        gain.reshape(1, width),
    )

    def piece(sums, at, size):
        return sums[at : at + size].astype(F32)

    return (
        new.reshape(latent.shape),
        flow.reshape(latent.shape),
        piece(sums_b, 0, width),
        piece(sums_b, width, width),
        piece(sums_a, 0, width),
        piece(sums_a, width, width),
        piece(sums_a, 2 * width, width),
        piece(sums_a, 3 * width, width),
        piece(sums_b, 2 * width, 3),
        piece(sums_b, 2 * width + 3, 1).reshape(width),
    )


def solution(mesh):
    cell_spec = P(("groups", "gx"), "gy", None, None)
    placed = (cell_spec, cell_spec, P(("groups", "gx"), "gy"), cell_spec) + (P(),) * 8
    return jax.shard_map(
        partial(per_device, mesh.shape["gx"], mesh.shape["gy"]),
        mesh=mesh,
        in_specs=placed,
        out_specs=(cell_spec, cell_spec) + (P("groups", None),) * 7 + (P("groups"),),
        check_vma=False,
    )
```

```python
from functools import partial

import jax
import jax.numpy as jnp
from jax import lax
from jax.experimental import pallas as pl
from jax.experimental.pallas import tpu as pltpu
from jax.sharding import PartitionSpec as P

STEPS = 2
EPSILON = 1e-05
OFFSETS = ((-1, -1), (-1, 0), (-1, 1), (0, -1), (0, 0), (0, 1), (1, -1), (1, 0), (1, 1))
SIDES = ((1, 0), (-1, 0), (0, 1), (0, -1), (1, 1), (1, -1), (-1, 1), (-1, -1))
MESH = pl.DeviceIdType.MESH
F32 = jnp.float32
BF16 = jnp.bfloat16
SEND_AT = 16
GEO_AT = 88
DEPTH = 128
UNROLL = 2


def round16(rows):
    return -(-rows // 16) * 16


def mm(a, b):
    return jnp.dot(a.astype(BF16), b.astype(BF16), preferred_element_type=F32)


def mm_t(a, b):
    return lax.dot_general(
        a.astype(BF16), b.astype(BF16), (((1,), (1,)), ((), ())), preferred_element_type=F32
    )


def outer(a, b):
    return lax.dot_general(
        a.astype(BF16), b.astype(BF16), (((0,), (0,)), ((), ())), preferred_element_type=F32
    )


def rounded(value):
    return value.astype(BF16).astype(F32)


def segments(cx, cy, slots):
    found, at = [], 0
    for dx, dy in SIDES:
        rows = round16((cx if dx == 0 else 1) * (cy if dy == 0 else 1) * slots)
        found.append((at, rows))
        at += rows
    return found, at


def span(step, size, low, high):
    if step == 0:
        return range(1, size + 1)
    return [high] if step == 1 else [low]


def kernel(
    ngx,
    ngy,
    cells_x,
    cells_y,
    h_ref,
    cell_ref,
    cot_ref,
    w_recv,
    w_send,
    w_msg,
    w_nh,
    w_nm,
    w_out,
    geom_ref,
    gain_ref,
    latent_out,
    grad_latent,
    out_a,
    out_b,
    out_few,
    ext,
    gext,
    recv,
    agg,
    g_agg,
    g_recv,
    hs,
    agg16,
    msg16,
    act16,
    hidden,
    xhat,
    rstd,
    acc,
    acc_small,
    acc_geo,
    pos_send,
    pos_recv,
    pos_ext,
    feat,
    geo,
    mat,
    mat_t,
    geo_b,
    halo_send,
    halo_recv,
    part_a,
    part_b,
    got_a,
    got_b,
    few,
    few_y,
    few_x,
    pos_sems,
    halo_sems,
    red_sems,
    few_sems,
):
    slots = 8
    cells = cells_x * cells_y
    pairs = 9 * slots * slots
    wide = geo.shape[-1]
    n = ngx * ngy
    gx, gy = lax.axis_index("gx"), lax.axis_index("gy")
    me = gx * ngy + gy
    width = h_ref.shape[1]
    segs, _ = segments(cells_x, cells_y, slots)

    def place(dx, dy):
        return {"gx": lax.rem(gx + dx + ngx, ngx), "gy": lax.rem(gy + dy + ngy, ngy)}

    def peer(k):
        other = lax.rem(me + k, n)
        return other, {"gx": lax.div(other, ngy), "gy": lax.rem(other, ngy)}

    barrier = pltpu.get_barrier_semaphore()

    def greet(k, carry):
        _, device = peer(k)
        pl.semaphore_signal(barrier, inc=1, device_id=device, device_id_type=MESH)
        return carry

    lax.fori_loop(1, n, greet, 0)

    def wait_all(ref, sem):
        pltpu.make_async_copy(ref, ref, sem).wait()

    by_cell = cell_ref[...]
    for d, (dx, dy) in enumerate(SIDES):
        xs = [x - 1 for x in span(dx, cells_x, 1, cells_x)]
        if dx != 0 and dy == 0:
            pos_send[d] = by_cell[xs[0]]
        else:
            y = 0 if dy == -1 else cells_y - 1
            rows = [by_cell[x, y : y + 1] for x in xs]
            rows += [rows[-1]] * (cells_y - len(rows))
            pos_send[d] = jnp.concatenate(rows, axis=0)

    h0 = h_ref[...]
    pl.semaphore_wait(barrier, n - 1)
    for d, (dx, dy) in enumerate(SIDES):
        pltpu.make_async_remote_copy(
            pos_send.at[d], pos_recv.at[d], pos_sems.at[0], pos_sems.at[1],
            device_id=place(dx, dy), device_id_type=MESH,
        ).start()

    def start_halo(phase, taken):
        for d, (dx, dy) in enumerate(SIDES):
            at, rows = segs[d]
            tiles = taken(dx, dy)
            tiles = tiles + [tiles[-1]] * (rows // slots - len(tiles))
            halo_send[phase, pl.ds(at, rows)] = jnp.concatenate(tiles, axis=0).astype(BF16)
            pltpu.make_async_remote_copy(
                halo_send.at[phase, pl.ds(at, rows)],
                halo_recv.at[phase, pl.ds(at, rows)],
                halo_sems.at[0, phase],
                halo_sems.at[1, phase],
                device_id=place(dx, dy),
                device_id_type=MESH,
            ).start()

    def end_halo(phase):
        wait_all(halo_recv.at[phase], halo_sems.at[1, phase])
        wait_all(halo_send.at[phase], halo_sems.at[0, phase])

    def project(step, h):
        hs[step] = h
        recv[step] = mm(h, w_recv[...]).reshape(cells, slots, width)
        half = (rounded(mm(h, w_send[...])) * 0.5).reshape(cells_x, cells_y, slots, width)

        def taken(dx, dy):
            return [
                half[x - 1, y - 1]
                for x in span(dx, cells_x, 1, cells_x)
                for y in span(dy, cells_y, 1, cells_y)
            ]

        start_halo(step, taken)
        for x in range(cells_x):
            ext[step, x + 1, pl.ds(1, cells_y)] = half[x]

    def arrive(step):
        end_halo(step)
        for d, (dx, dy) in enumerate(SIDES):
            at, rows = segs[d]
            block = halo_recv[step, pl.ds(at, rows)].astype(F32)
            where = [
                (x, y)
                for x in span(dx, cells_x, cells_x + 1, 0)
                for y in span(dy, cells_y, cells_y + 1, 0)
            ]
            for t, (x, y) in enumerate(where):
                ext[step, x, y] = block[t * slots : (t + 1) * slots]

    project(0, h0)

    g = geom_ref[...] * 0.5
    g_hi = rounded(g)
    g_lo = g - g_hi
    rows = []
    for f in range(3):
        rows += [g_hi[f : f + 1], g_hi[f : f + 1], g_lo[f : f + 1]]
    rows.append(jnp.zeros((DEPTH - GEO_AT - 9, width), F32))
    geo_b[...] = jnp.concatenate(rows, axis=0)

    k_at = lax.broadcasted_iota(jnp.int32, (DEPTH, wide), 0)
    r_at = lax.broadcasted_iota(jnp.int32, (DEPTH, wide), 1)
    takes_recv = (k_at < SEND_AT) & ((r_at & 7) == (k_at & 7))
    takes_send = (k_at >= SEND_AT) & (k_at < GEO_AT) & ((r_at >> 3) == k_at - SEND_AT)
    one_hot = jnp.where((r_at < pairs) & (takes_recv | takes_send), 1.0, 0.0).astype(F32)
    lane = lax.broadcasted_iota(jnp.int32, (1, wide), 1)
    cell_o = lane >> 6
    third = (cell_o >= 3).astype(jnp.int32) + (cell_o >= 6).astype(jnp.int32)
    off_x = (third - 1).astype(F32)
    off_y = (cell_o - third * 3 - 1).astype(F32)
    same = (cell_o == 4) & (((lane >> 3) & 7) == (lane & 7))

    wait_all(pos_recv, pos_sems.at[1])
    wait_all(pos_send, pos_sems.at[0])
    for x in range(cells_x):
        pos_ext[x + 1, pl.ds(1, cells_y)] = by_cell[x]
    for d, (dx, dy) in enumerate(SIDES):
        tile = pos_recv[d]
        xs = list(span(dx, cells_x, cells_x + 1, 0))
        if dx != 0 and dy == 0:
            pos_ext[xs[0], pl.ds(1, cells_y)] = tile
        else:
            y = 0 if dy == 1 else cells_y + 1
            for t, x in enumerate(xs):
                pos_ext[x, pl.ds(y, 1)] = tile[t : t + 1]
    feat[...] = jnp.zeros(feat.shape, F32)
    for x in range(cells_x):
        rows_x = pl.ds(x * cells_y, cells_y)
        for f in range(3):
            own = by_cell[x][:, f * slots : (f + 1) * slots]
            feat[f, rows_x, 0:slots] = own if f == 2 else -own
        for o, (ox, oy) in enumerate(OFFSETS):
            near = pos_ext[x + 1 + ox, pl.ds(1 + oy, cells_y)]
            at = SEND_AT + o * slots
            for f in range(3):
                feat[f, rows_x, at : at + slots] = near[:, f * slots : (f + 1) * slots]
    disp_x = mm(feat[0], one_hot) + off_x
    disp_y = mm(feat[1], one_hot) + off_y
    both = mm(feat[2], one_hot)
    dist = disp_x * disp_x + disp_y * disp_y
    wgt = jnp.where((both > 1.5) & jnp.logical_not(same), 1.0 / (1.0 + dist), 0.0)
    for f, value in enumerate((disp_x, disp_y, dist, wgt)):
        geo[f] = value
    row16 = lax.broadcasted_iota(jnp.int32, (16, wide), 0)
    rest = jnp.zeros((DEPTH - GEO_AT - 16, wide), F32)

    def prepare(c, carry):
        w = geo[3, pl.ds(c, 1)]
        w_hi = rounded(w)
        tile = jnp.zeros((16, wide), F32)
        tile_w = jnp.zeros((16, wide), F32)
        for f in range(3):
            value = geo[f, pl.ds(c, 1)]
            hi = rounded(value)
            at = 3 * f
            tile = jnp.where((row16 == at) | (row16 == at + 2), hi, tile)
            tile = jnp.where(row16 == at + 1, value - hi, tile)
            value = value * w
            hi = rounded(value)
            tile_w = jnp.where(row16 == at, hi, tile_w)
            tile_w = jnp.where(row16 == at + 1, value - hi, tile_w)
        full = jnp.concatenate([one_hot[:GEO_AT], tile, rest], axis=0)
        mat[c] = full.T[:pairs].astype(BF16)
        full_w = jnp.concatenate(
            [
                one_hot[:slots] * w_hi,
                one_hot[slots:SEND_AT] * (w - w_hi),
                one_hot[SEND_AT:GEO_AT] * w,
                tile_w,
                rest,
            ],
            axis=0,
        )
        mat_t[c] = full_w[:, :pairs].astype(BF16)
        return carry

    lax.fori_loop(0, cells, prepare, 0)

    def half_preact(step, x, y):
        c = x * cells_y + y
        r = recv[step, c] * 0.5
        hi = rounded(r)
        tiles = [hi, r - hi]
        tiles += [ext[step, x + 1 + ox, y + 1 + oy] for ox, oy in OFFSETS]
        b = jnp.concatenate(tiles + [geo_b[...]], axis=0).astype(BF16)
        return jnp.dot(mat[c], b, preferred_element_type=F32).astype(BF16)

    def inner_cells(body):
        across = cells_y - 2

        def one(i, carry):
            body(1 + lax.div(i, across), 1 + lax.rem(i, across))
            return carry

        lax.fori_loop(0, (cells_x - 2) * across, one, 0, unroll=UNROLL)

    def edge_cells(body):
        def row(i, carry):
            body(lax.div(i, cells_y) * (cells_x - 1), lax.rem(i, cells_y))
            return carry

        def column(i, carry):
            body(1 + lax.div(i, 2), lax.rem(i, 2) * (cells_y - 1))
            return carry

        lax.fori_loop(0, 2 * cells_y, row, 0, unroll=UNROLL)
        lax.fori_loop(0, 2 * (cells_x - 2), column, 0, unroll=UNROLL)

    def forward_cell(step, x, y):
        c = x * cells_y + y
        q = half_preact(step, x, y)
        both_parts = jnp.dot(
            mat_t[c, :SEND_AT], q + q * jnp.tanh(q), preferred_element_type=F32
        )
        agg[c] = both_parts[:slots] + both_parts[slots:]

    def backward_cell(step, x, y):
        c = x * cells_y + y
        q = half_preact(step, x, y).reshape(-1, 2 * slots, width)
        up = g_agg[c] * 0.5
        up = jnp.concatenate([up, up], axis=0).astype(BF16)[None]
        t = jnp.tanh(q)
        d = up * ((1.0 + t) * (1.0 + (q - q * t)))
        back = jnp.dot(mat_t[c], d.reshape(pairs, width), preferred_element_type=F32)
        g_recv[c] = back[:slots] + back[slots:SEND_AT]
        for o, (ox, oy) in enumerate(OFFSETS):
            at = SEND_AT + o * slots
            gext[x + 1 + ox, y + 1 + oy] += back[at : at + slots]
        acc_geo[...] += back[GEO_AT : GEO_AT + 16]

    gain = gain_ref[...]

    def node_forward(step):
        a16 = agg[...].reshape(cells * slots, width).astype(BF16)
        agg16[step] = a16
        m16 = mm(a16, w_msg[...]).astype(BF16)
        msg16[step] = m16
        hid = mm(hs[step], w_nh[...]) + mm(m16, w_nm[...])
        hidden[step] = hid
        half = hid * 0.5
        a = (half + half * jnp.tanh(half)).astype(BF16)
        act16[step] = a
        out = mm(a, w_out[...])
        center = out - jnp.mean(out, axis=-1, keepdims=True)
        scale = lax.rsqrt(jnp.mean(center * center, axis=-1, keepdims=True) + EPSILON)
        normed = center * scale
        xhat[step] = normed
        rstd[step] = jnp.broadcast_to(scale, rstd.shape[1:])
        return (hs[step].astype(F32) + normed * gain).astype(BF16)

    for step in range(STEPS):
        inner_cells(partial(forward_cell, step))
        arrive(step)
        edge_cells(partial(forward_cell, step))
        if step == 0:
            project(1, node_forward(0))
    latent_out[...] = node_forward(1)

    def spread_out(part, got, share, sem):
        def one(k, carry):
            other, device = peer(k)
            pltpu.make_async_remote_copy(
                part.at[pl.ds(pl.multiple_of(other * share, 16), share)],
                got.at[k - 1],
                red_sems.at[0, sem],
                red_sems.at[1, sem],
                device_id=device,
                device_id_type=MESH,
            ).start()
            return carry

        lax.fori_loop(1, n, one, 0)

    def gather_in(part, got, share, result, sem):
        wait_all(got, red_sems.at[1, sem])
        wait_all(got, red_sems.at[0, sem])
        mine = pl.ds(pl.multiple_of(me * share, 16), share)
        total = lax.fori_loop(
            0, n - 1, lambda k, t: t + got[k].astype(F32), part[mine].astype(F32)
        )
        result[mine] = total.astype(BF16)

        def one(k, carry):
            _, device = peer(k)
            pltpu.make_async_remote_copy(
                result.at[mine], result.at[mine], red_sems.at[0, sem + 1],
                red_sems.at[1, sem + 1], device_id=device, device_id_type=MESH,
            ).start()
            return carry

        lax.fori_loop(1, n, one, 0)

    def gathered(share, result, sem):
        size = result.at[pl.ds(0, (n - 1) * share)]
        wait_all(size, red_sems.at[1, sem + 1])
        wait_all(size, red_sems.at[0, sem + 1])

    def sum_few_start(stage, axis, size, here, got):
        for k in range(1, size):
            pltpu.make_async_remote_copy(
                few.at[stage], got.at[k - 1], few_sems.at[0, stage], few_sems.at[1, stage],
                device_id={axis: lax.rem(here + k, size)}, device_id_type=MESH,
            ).start()

    def sum_few_end(stage, got):
        wait_all(got, few_sems.at[1, stage])
        wait_all(got, few_sems.at[0, stage])
        few[stage + 1] = few[stage] + jnp.sum(got[...], axis=0)

    share_a = got_a.shape[1]
    share_b = got_b.shape[1]

    flow = cot_ref[...]
    acc_geo[...] = jnp.zeros(acc_geo.shape, F32)
    for step in (1, 0):
        last = step == 0

        def put(index, term):
            if not last:
                acc[index] = term
                return
            term = (acc[index] + term).astype(BF16)
            if index < 4:
                part_a[pl.ds(index * width, width)] = term
            else:
                part_b[pl.ds((index - 4) * width, width)] = term

        flow32 = flow.astype(F32)
        normed = xhat[step]
        g_gain = jnp.sum(flow32 * normed, axis=0, keepdims=True)
        if last:
            g_gain = g_gain + acc_small[0:1]
        acc_small[...] = jnp.broadcast_to(g_gain, acc_small.shape)
        scaled = flow32 * gain
        d_out = rstd[step][:, :1] * (
            scaled
            - jnp.mean(scaled, axis=-1, keepdims=True)
            - normed * jnp.mean(scaled * normed, axis=-1, keepdims=True)
        )
        put(3, outer(act16[step], d_out))
        d_act = rounded(mm_t(d_out, w_out[...]))
        half = hidden[step] * 0.5
        t = jnp.tanh(half)
        d_hid = (d_act * 0.5) * ((1.0 + t) * (1.0 + (half - half * t)))
        put(1, outer(hs[step], d_hid))
        put(2, outer(msg16[step], d_hid))
        d_msg = mm_t(d_hid, w_nm[...]).astype(BF16)
        put(0, outer(agg16[step], d_msg))
        if last:
            if part_a.shape[0] > 4 * width:
                part_a[pl.ds(4 * width, part_a.shape[0] - 4 * width)] = jnp.zeros(
                    (part_a.shape[0] - 4 * width, width), BF16
                )
            spread_out(part_a, got_a, share_a, 0)
        g_agg[...] = rounded(mm_t(d_msg, w_msg[...])).reshape(cells, slots, width)
        gext[...] = jnp.zeros(gext.shape, F32)
        edge_cells(partial(backward_cell, step))

        def taken(dx, dy):
            return [
                gext[x, y]
                for x in span(dx, cells_x, 0, cells_x + 1)
                for y in span(dy, cells_y, 0, cells_y + 1)
            ]

        start_halo(STEPS + step, taken)
        if last:
            gather_in(part_a, got_a, share_a, out_a, 0)
        inner_cells(partial(backward_cell, step))
        if last:
            sums = acc_geo[...]
            tail = [sums[3 * f : 3 * f + 1] + sums[3 * f + 1 : 3 * f + 2] for f in range(3)]
            tail += [acc_small[0:1], jnp.zeros((4, width), F32)]
            few[0] = jnp.concatenate(tail, axis=0)
            sum_few_start(0, "gy", ngy, gy, few_y)
        d_recv = g_recv[...].reshape(cells * slots, width)
        put(4, outer(hs[step], d_recv))
        d_h = flow32 + rounded(mm_t(d_hid, w_nh[...])) + rounded(mm_t(d_recv, w_recv[...]))
        end_halo(STEPS + step)
        for d, (dx, dy) in enumerate(SIDES):
            at, rows_d = segs[d]
            arrived = halo_recv[STEPS + step, pl.ds(at, rows_d)].astype(F32)
            where = [
                (x, y)
                for x in span(dx, cells_x, cells_x, 1)
                for y in span(dy, cells_y, cells_y, 1)
            ]
            for i, (x, y) in enumerate(where):
                gext[x, y] += arrived[i * slots : (i + 1) * slots]
        d_send = jnp.concatenate(
            [
                gext[x + 1, pl.ds(1, cells_y)].reshape(cells_y * slots, width)
                for x in range(cells_x)
            ],
            axis=0,
        ).astype(BF16)
        put(5, outer(hs[step], d_send))
        if last:
            if part_b.shape[0] > 2 * width:
                part_b[pl.ds(2 * width, part_b.shape[0] - 2 * width)] = jnp.zeros(
                    (part_b.shape[0] - 2 * width, width), BF16
                )
            spread_out(part_b, got_b, share_b, 2)
            sum_few_end(0, few_y)
            sum_few_start(1, "gx", ngx, gx, few_x)
        flow = (d_h + rounded(mm_t(d_send, w_send[...]))).astype(BF16)
    grad_latent[...] = flow
    gather_in(part_b, got_b, share_b, out_b, 2)
    sum_few_end(1, few_x)
    out_few[...] = few[2]
    gathered(share_a, out_a, 0)
    gathered(share_b, out_b, 2)


def per_device(
    ngx,
    ngy,
    latent,
    positions,
    counts,
    cotangent,
    w_recv,
    w_send,
    w_msg,
    w_node_h,
    w_node_m,
    w_out,
    geometry,
    gain,
):
    cells_x, cells_y, slots, width = latent.shape
    cells = cells_x * cells_y
    rows = cells * slots
    n = ngx * ngy
    slot_index = lax.broadcasted_iota(jnp.int32, (cells_x, cells_y, slots), 2)
    validity = (slot_index < counts[:, :, None]).astype(F32)
    by_cell = jnp.concatenate(
        [
            positions[..., 0].astype(F32),
            positions[..., 1].astype(F32),
            validity,
            jnp.zeros((cells_x, cells_y, 128 - 3 * slots), F32),
        ],
        axis=-1,
    )
    pairs = 9 * slots * slots
    wide = -(-pairs // 128) * 128
    _, halo_rows = segments(cells_x, cells_y, slots)
    share_a = round16(-(-4 * width // n))
    share_b = round16(-(-2 * width // n))
    vmem = pltpu.VMEM
    scratch = [
        vmem((STEPS, cells_x + 2, cells_y + 2, slots, width), F32),
        vmem((cells_x + 2, cells_y + 2, slots, width), F32),
        vmem((STEPS, cells, slots, width), F32),
        vmem((cells, slots, width), F32),
        vmem((cells, slots, width), F32),
        vmem((cells, slots, width), F32),
        vmem((STEPS, rows, width), BF16),
        vmem((STEPS, rows, width), BF16),
        vmem((STEPS, rows, width), BF16),
        vmem((STEPS, rows, width), BF16),
        vmem((STEPS, rows, width), F32),
        vmem((STEPS, rows, width), F32),
        vmem((STEPS, rows, 128), F32),
        vmem((6, width, width), F32),
        vmem((8, width), F32),
        vmem((16, width), F32),
        vmem((8, cells_y, 128), F32),
        vmem((8, cells_y, 128), F32),
        vmem((cells_x + 2, -(-(cells_y + 2) // 8) * 8, 128), F32),
        vmem((3, cells, 128), F32),
        vmem((4, cells, wide), F32),
        vmem((cells, pairs, DEPTH), BF16),
        vmem((cells, DEPTH, pairs), BF16),
        vmem((DEPTH - GEO_AT, width), F32),
        vmem((2 * STEPS, halo_rows, width), BF16),
        vmem((2 * STEPS, halo_rows, width), BF16),
        vmem((n * share_a, width), BF16),
        vmem((n * share_b, width), BF16),
        vmem((n - 1, share_a, width), BF16),
        vmem((n - 1, share_b, width), BF16),
        vmem((3, 8, width), F32),
        vmem((ngy - 1, 8, width), F32),
        vmem((ngx - 1, 8, width), F32),
        pltpu.SemaphoreType.DMA((2,)),
        pltpu.SemaphoreType.DMA((2, 2 * STEPS)),
        pltpu.SemaphoreType.DMA((2, 4)),
        pltpu.SemaphoreType.DMA((2, 2)),
    ]
    spec = pl.BlockSpec(memory_space=pltpu.VMEM)
    new, flow, sums_a, sums_b, sums_few = pl.pallas_call(
        partial(kernel, ngx, ngy, cells_x, cells_y),
        out_shape=[
            jax.ShapeDtypeStruct((rows, width), BF16),
            jax.ShapeDtypeStruct((rows, width), BF16),
            jax.ShapeDtypeStruct((n * share_a, width), BF16),
            jax.ShapeDtypeStruct((n * share_b, width), BF16),
            jax.ShapeDtypeStruct((8, width), F32),
        ],
        in_specs=[spec] * 11,
        out_specs=[spec] * 5,
        scratch_shapes=scratch,
        compiler_params=pltpu.CompilerParams(
            collective_id=0, has_side_effects=True, vmem_limit_bytes=56 * 2**20
        ),
        name="evolver",
    )(
        latent.reshape(rows, width),
        by_cell,
        cotangent.reshape(rows, width),
        w_recv,
        w_send,
        w_msg,
        w_node_h,
        w_node_m,
        w_out,
        geometry,
        gain.reshape(1, width),
    )

    def piece(sums, at, size):
        return sums[at : at + size].astype(F32)

    return (
        new.reshape(latent.shape),
        flow.reshape(latent.shape),
        piece(sums_b, 0, width),
        piece(sums_b, width, width),
        piece(sums_a, 0, width),
        piece(sums_a, width, width),
        piece(sums_a, 2 * width, width),
        piece(sums_a, 3 * width, width),
        sums_few[:3],
        sums_few[3],
    )


def solution(mesh):
    cell_spec = P(("groups", "gx"), "gy", None, None)
    placed = (cell_spec, cell_spec, P(("groups", "gx"), "gy"), cell_spec) + (P(),) * 8
    return jax.shard_map(
        partial(per_device, mesh.shape["gx"], mesh.shape["gy"]),
        mesh=mesh,
        in_specs=placed,
        out_specs=(cell_spec, cell_spec) + (P("groups", None),) * 7 + (P("groups"),),
        check_vma=False,
    )
```

```python
from functools import partial

import jax
import jax.numpy as jnp
from jax import lax
from jax.experimental import pallas as pl
from jax.experimental.pallas import tpu as pltpu
from jax.sharding import PartitionSpec as P

STEPS = 2
EPSILON = 1e-05
OFFSETS = ((-1, -1), (-1, 0), (-1, 1), (0, -1), (0, 0), (0, 1), (1, -1), (1, 0), (1, 1))
SIDES = ((1, 0), (-1, 0), (0, 1), (0, -1), (1, 1), (1, -1), (-1, 1), (-1, -1))
MESH = pl.DeviceIdType.MESH
F32 = jnp.float32
BF16 = jnp.bfloat16
SEND_AT = 16
GEO_AT = 88
DEPTH = 128
UNROLL = 4


def round16(rows):
    return -(-rows // 16) * 16


def mm(a, b):
    return jnp.dot(a.astype(BF16), b.astype(BF16), preferred_element_type=F32)


def mm_t(a, b):
    return lax.dot_general(
        a.astype(BF16), b.astype(BF16), (((1,), (1,)), ((), ())), preferred_element_type=F32
    )


def outer(a, b):
    return lax.dot_general(
        a.astype(BF16), b.astype(BF16), (((0,), (0,)), ((), ())), preferred_element_type=F32
    )


def rounded(value):
    return value.astype(BF16).astype(F32)


def segments(cx, cy, slots):
    found, at = [], 0
    for dx, dy in SIDES:
        rows = round16((cx if dx == 0 else 1) * (cy if dy == 0 else 1) * slots)
        found.append((at, rows))
        at += rows
    return found, at


def span(step, size, low, high):
    if step == 0:
        return range(1, size + 1)
    return [high] if step == 1 else [low]


def kernel(
    ngx,
    ngy,
    cells_x,
    cells_y,
    h_ref,
    cell_ref,
    cot_ref,
    w_recv,
    w_send,
    w_msg,
    w_nh,
    w_nm,
    w_out,
    geom_ref,
    gain_ref,
    latent_out,
    grad_latent,
    out_a,
    out_b,
    out_few,
    ext,
    gext,
    recv,
    agg,
    g_agg,
    g_recv,
    hs,
    agg16,
    msg16,
    act16,
    hidden,
    xhat,
    rstd,
    acc,
    acc_small,
    acc_geo,
    pos_send,
    pos_recv,
    pos_ext,
    feat,
    geo,
    mat,
    mat_t,
    geo_b,
    halo_send,
    halo_recv,
    part_a,
    part_b,
    got_a,
    got_b,
    few,
    few_y,
    few_x,
    pos_sems,
    halo_sems,
    red_sems,
    few_sems,
):
    slots = 8
    cells = cells_x * cells_y
    pairs = 9 * slots * slots
    wide = geo.shape[-1]
    n = ngx * ngy
    gx, gy = lax.axis_index("gx"), lax.axis_index("gy")
    me = gx * ngy + gy
    width = h_ref.shape[1]
    segs, _ = segments(cells_x, cells_y, slots)

    def place(dx, dy):
        return {"gx": lax.rem(gx + dx + ngx, ngx), "gy": lax.rem(gy + dy + ngy, ngy)}

    def peer(k):
        other = lax.rem(me + k, n)
        return other, {"gx": lax.div(other, ngy), "gy": lax.rem(other, ngy)}

    barrier = pltpu.get_barrier_semaphore()

    def greet(k, carry):
        _, device = peer(k)
        pl.semaphore_signal(barrier, inc=1, device_id=device, device_id_type=MESH)
        return carry

    lax.fori_loop(1, n, greet, 0)

    def wait_all(ref, sem):
        pltpu.make_async_copy(ref, ref, sem).wait()

    by_cell = cell_ref[...]
    for d, (dx, dy) in enumerate(SIDES):
        xs = [x - 1 for x in span(dx, cells_x, 1, cells_x)]
        if dx != 0 and dy == 0:
            pos_send[d] = by_cell[xs[0]]
        else:
            y = 0 if dy == -1 else cells_y - 1
            rows = [by_cell[x, y : y + 1] for x in xs]
            rows += [rows[-1]] * (cells_y - len(rows))
            pos_send[d] = jnp.concatenate(rows, axis=0)

    h0 = h_ref[...]
    pl.semaphore_wait(barrier, n - 1)
    for d, (dx, dy) in enumerate(SIDES):
        pltpu.make_async_remote_copy(
            pos_send.at[d], pos_recv.at[d], pos_sems.at[0], pos_sems.at[1],
            device_id=place(dx, dy), device_id_type=MESH,
        ).start()

    def start_halo(phase, taken):
        for d, (dx, dy) in enumerate(SIDES):
            at, rows = segs[d]
            tiles = taken(dx, dy)
            tiles = tiles + [tiles[-1]] * (rows // slots - len(tiles))
            halo_send[phase, pl.ds(at, rows)] = jnp.concatenate(tiles, axis=0).astype(BF16)
            pltpu.make_async_remote_copy(
                halo_send.at[phase, pl.ds(at, rows)],
                halo_recv.at[phase, pl.ds(at, rows)],
                halo_sems.at[0, phase],
                halo_sems.at[1, phase],
                device_id=place(dx, dy),
                device_id_type=MESH,
            ).start()

    def end_halo(phase):
        wait_all(halo_recv.at[phase], halo_sems.at[1, phase])
        wait_all(halo_send.at[phase], halo_sems.at[0, phase])

    def project(step, h):
        hs[step] = h
        recv[step] = mm(h, w_recv[...]).reshape(cells, slots, width)
        half = (rounded(mm(h, w_send[...])) * 0.5).reshape(cells_x, cells_y, slots, width)

        def taken(dx, dy):
            return [
                half[x - 1, y - 1]
                for x in span(dx, cells_x, 1, cells_x)
                for y in span(dy, cells_y, 1, cells_y)
            ]

        start_halo(step, taken)
        for x in range(cells_x):
            ext[step, x + 1, pl.ds(1, cells_y)] = half[x]

    def arrive(step):
        end_halo(step)
        for d, (dx, dy) in enumerate(SIDES):
            at, rows = segs[d]
            block = halo_recv[step, pl.ds(at, rows)].astype(F32)
            where = [
                (x, y)
                for x in span(dx, cells_x, cells_x + 1, 0)
                for y in span(dy, cells_y, cells_y + 1, 0)
            ]
            for t, (x, y) in enumerate(where):
                ext[step, x, y] = block[t * slots : (t + 1) * slots]

    project(0, h0)

    g = geom_ref[...] * 0.5
    g_hi = rounded(g)
    g_lo = g - g_hi
    rows = []
    for f in range(3):
        rows += [g_hi[f : f + 1], g_hi[f : f + 1], g_lo[f : f + 1]]
    rows.append(jnp.zeros((DEPTH - GEO_AT - 9, width), F32))
    geo_b[...] = jnp.concatenate(rows, axis=0)

    k_at = lax.broadcasted_iota(jnp.int32, (DEPTH, wide), 0)
    r_at = lax.broadcasted_iota(jnp.int32, (DEPTH, wide), 1)
    takes_recv = (k_at < SEND_AT) & ((r_at & 7) == (k_at & 7))
    takes_send = (k_at >= SEND_AT) & (k_at < GEO_AT) & ((r_at >> 3) == k_at - SEND_AT)
    one_hot = jnp.where((r_at < pairs) & (takes_recv | takes_send), 1.0, 0.0).astype(F32)
    lane = lax.broadcasted_iota(jnp.int32, (1, wide), 1)
    cell_o = lane >> 6
    third = (cell_o >= 3).astype(jnp.int32) + (cell_o >= 6).astype(jnp.int32)
    off_x = (third - 1).astype(F32)
    off_y = (cell_o - third * 3 - 1).astype(F32)
    same = (cell_o == 4) & (((lane >> 3) & 7) == (lane & 7))

    wait_all(pos_recv, pos_sems.at[1])
    wait_all(pos_send, pos_sems.at[0])
    for x in range(cells_x):
        pos_ext[x + 1, pl.ds(1, cells_y)] = by_cell[x]
    for d, (dx, dy) in enumerate(SIDES):
        tile = pos_recv[d]
        xs = list(span(dx, cells_x, cells_x + 1, 0))
        if dx != 0 and dy == 0:
            pos_ext[xs[0], pl.ds(1, cells_y)] = tile
        else:
            y = 0 if dy == 1 else cells_y + 1
            for t, x in enumerate(xs):
                pos_ext[x, pl.ds(y, 1)] = tile[t : t + 1]
    feat[...] = jnp.zeros(feat.shape, F32)
    for x in range(cells_x):
        rows_x = pl.ds(x * cells_y, cells_y)
        for f in range(3):
            own = by_cell[x][:, f * slots : (f + 1) * slots]
            feat[f, rows_x, 0:slots] = own if f == 2 else -own
        for o, (ox, oy) in enumerate(OFFSETS):
            near = pos_ext[x + 1 + ox, pl.ds(1 + oy, cells_y)]
            at = SEND_AT + o * slots
            for f in range(3):
                feat[f, rows_x, at : at + slots] = near[:, f * slots : (f + 1) * slots]
    disp_x = mm(feat[0], one_hot) + off_x
    disp_y = mm(feat[1], one_hot) + off_y
    both = mm(feat[2], one_hot)
    dist = disp_x * disp_x + disp_y * disp_y
    wgt = jnp.where((both > 1.5) & jnp.logical_not(same), 1.0 / (1.0 + dist), 0.0)
    for f, value in enumerate((disp_x, disp_y, dist, wgt)):
        geo[f] = value
    row16 = lax.broadcasted_iota(jnp.int32, (16, wide), 0)
    rest = jnp.zeros((DEPTH - GEO_AT - 16, wide), F32)

    def prepare(c, carry):
        w = geo[3, pl.ds(c, 1)]
        w_hi = rounded(w)
        tile = jnp.zeros((16, wide), F32)
        tile_w = jnp.zeros((16, wide), F32)
        for f in range(3):
            value = geo[f, pl.ds(c, 1)]
            hi = rounded(value)
            at = 3 * f
            tile = jnp.where((row16 == at) | (row16 == at + 2), hi, tile)
            tile = jnp.where(row16 == at + 1, value - hi, tile)
            value = value * w
            hi = rounded(value)
            tile_w = jnp.where(row16 == at, hi, tile_w)
            tile_w = jnp.where(row16 == at + 1, value - hi, tile_w)
        full = jnp.concatenate([one_hot[:GEO_AT], tile, rest], axis=0)
        mat[c] = full.T[:pairs].astype(BF16)
        full_w = jnp.concatenate(
            [
                one_hot[:slots] * w_hi,
                one_hot[slots:SEND_AT] * (w - w_hi),
                one_hot[SEND_AT:GEO_AT] * w,
                tile_w,
                rest,
            ],
            axis=0,
        )
        mat_t[c] = full_w[:, :pairs].astype(BF16)
        return carry

    lax.fori_loop(0, cells, prepare, 0, unroll=UNROLL)

    def half_preact(step, x, y):
        c = x * cells_y + y
        r = recv[step, c] * 0.5
        hi = rounded(r)
        tiles = [hi, r - hi]
        tiles += [ext[step, x + 1 + ox, y + 1 + oy] for ox, oy in OFFSETS]
        b = jnp.concatenate(tiles + [geo_b[...]], axis=0).astype(BF16)
        return jnp.dot(mat[c], b, preferred_element_type=F32)

    def inner_cells(body):
        across = cells_y - 2

        def one(i, carry):
            body(1 + lax.div(i, across), 1 + lax.rem(i, across))
            return carry

        lax.fori_loop(0, (cells_x - 2) * across, one, 0, unroll=UNROLL)

    def edge_cells(body):
        def row(i, carry):
            body(lax.div(i, cells_y) * (cells_x - 1), lax.rem(i, cells_y))
            return carry

        def column(i, carry):
            body(1 + lax.div(i, 2), lax.rem(i, 2) * (cells_y - 1))
            return carry

        lax.fori_loop(0, 2 * cells_y, row, 0, unroll=UNROLL)
        lax.fori_loop(0, 2 * (cells_x - 2), column, 0, unroll=UNROLL)

    def forward_cell(step, x, y):
        c = x * cells_y + y
        q = half_preact(step, x, y)
        both_parts = jnp.dot(
            mat_t[c, :SEND_AT], (q + q * jnp.tanh(q)).astype(BF16), preferred_element_type=F32
        )
        agg[c] = both_parts[:slots] + both_parts[slots:]

    def backward_cell(step, x, y):
        c = x * cells_y + y
        q = half_preact(step, x, y).astype(BF16).reshape(-1, 2 * slots, width)
        up = g_agg[c] * 0.5
        up = jnp.concatenate([up, up], axis=0).astype(BF16)[None]
        t = jnp.tanh(q)
        d = up * ((1.0 + t) * (1.0 + (q - q * t)))
        back = jnp.dot(mat_t[c], d.reshape(pairs, width), preferred_element_type=F32)
        g_recv[c] = back[:slots] + back[slots:SEND_AT]
        for o, (ox, oy) in enumerate(OFFSETS):
            at = SEND_AT + o * slots
            gext[x + 1 + ox, y + 1 + oy] += back[at : at + slots]
        acc_geo[...] += back[GEO_AT : GEO_AT + 16]

    gain = gain_ref[...]

    def node_forward(step):
        a16 = agg[...].reshape(cells * slots, width).astype(BF16)
        agg16[step] = a16
        m16 = mm(a16, w_msg[...]).astype(BF16)
        msg16[step] = m16
        hid = mm(hs[step], w_nh[...]) + mm(m16, w_nm[...])
        hidden[step] = hid
        half = hid * 0.5
        a = (half + half * jnp.tanh(half)).astype(BF16)
        act16[step] = a
        out = mm(a, w_out[...])
        center = out - jnp.mean(out, axis=-1, keepdims=True)
        scale = lax.rsqrt(jnp.mean(center * center, axis=-1, keepdims=True) + EPSILON)
        normed = center * scale
        xhat[step] = normed
        rstd[step] = jnp.broadcast_to(scale, rstd.shape[1:])
        return (hs[step].astype(F32) + normed * gain).astype(BF16)

    for step in range(STEPS):
        inner_cells(partial(forward_cell, step))
        arrive(step)
        edge_cells(partial(forward_cell, step))
        if step == 0:
            project(1, node_forward(0))
    latent_out[...] = node_forward(1)

    def spread_out(part, got, share, sem):
        def one(k, carry):
            other, device = peer(k)
            pltpu.make_async_remote_copy(
                part.at[pl.ds(pl.multiple_of(other * share, 16), share)],
                got.at[k - 1],
                red_sems.at[0, sem],
                red_sems.at[1, sem],
                device_id=device,
                device_id_type=MESH,
            ).start()
            return carry

        lax.fori_loop(1, n, one, 0)

    def gather_in(part, got, share, result, sem):
        wait_all(got, red_sems.at[1, sem])
        wait_all(got, red_sems.at[0, sem])
        mine = pl.ds(pl.multiple_of(me * share, 16), share)
        total = lax.fori_loop(
            0, n - 1, lambda k, t: t + got[k].astype(F32), part[mine].astype(F32)
        )
        result[mine] = total.astype(BF16)

        def one(k, carry):
            _, device = peer(k)
            pltpu.make_async_remote_copy(
                result.at[mine], result.at[mine], red_sems.at[0, sem + 1],
                red_sems.at[1, sem + 1], device_id=device, device_id_type=MESH,
            ).start()
            return carry

        lax.fori_loop(1, n, one, 0)

    def gathered(share, result, sem):
        size = result.at[pl.ds(0, (n - 1) * share)]
        wait_all(size, red_sems.at[1, sem + 1])
        wait_all(size, red_sems.at[0, sem + 1])

    def sum_few_start(stage, axis, size, here, got):
        for k in range(1, size):
            pltpu.make_async_remote_copy(
                few.at[stage], got.at[k - 1], few_sems.at[0, stage], few_sems.at[1, stage],
                device_id={axis: lax.rem(here + k, size)}, device_id_type=MESH,
            ).start()

    def sum_few_end(stage, got):
        wait_all(got, few_sems.at[1, stage])
        wait_all(got, few_sems.at[0, stage])
        few[stage + 1] = few[stage] + jnp.sum(got[...], axis=0)

    share_a = got_a.shape[1]
    share_b = got_b.shape[1]

    flow = cot_ref[...]
    acc_geo[...] = jnp.zeros(acc_geo.shape, F32)
    for step in (1, 0):
        last = step == 0

        def put(index, term):
            if not last:
                acc[index] = term
                return
            term = (acc[index] + term).astype(BF16)
            if index < 4:
                part_a[pl.ds(index * width, width)] = term
            else:
                part_b[pl.ds((index - 4) * width, width)] = term

        flow32 = flow.astype(F32)
        normed = xhat[step]
        g_gain = jnp.sum(flow32 * normed, axis=0, keepdims=True)
        if last:
            g_gain = g_gain + acc_small[0:1]
        acc_small[...] = jnp.broadcast_to(g_gain, acc_small.shape)
        scaled = flow32 * gain
        d_out = rstd[step][:, :1] * (
            scaled
            - jnp.mean(scaled, axis=-1, keepdims=True)
            - normed * jnp.mean(scaled * normed, axis=-1, keepdims=True)
        )
        put(3, outer(act16[step], d_out))
        d_act = rounded(mm_t(d_out, w_out[...]))
        half = hidden[step] * 0.5
        t = jnp.tanh(half)
        d_hid = (d_act * 0.5) * ((1.0 + t) * (1.0 + (half - half * t)))
        put(1, outer(hs[step], d_hid))
        put(2, outer(msg16[step], d_hid))
        d_msg = mm_t(d_hid, w_nm[...]).astype(BF16)
        put(0, outer(agg16[step], d_msg))
        if last:
            if part_a.shape[0] > 4 * width:
                part_a[pl.ds(4 * width, part_a.shape[0] - 4 * width)] = jnp.zeros(
                    (part_a.shape[0] - 4 * width, width), BF16
                )
            spread_out(part_a, got_a, share_a, 0)
        g_agg[...] = rounded(mm_t(d_msg, w_msg[...])).reshape(cells, slots, width)
        gext[...] = jnp.zeros(gext.shape, F32)
        edge_cells(partial(backward_cell, step))

        def taken(dx, dy):
            return [
                gext[x, y]
                for x in span(dx, cells_x, 0, cells_x + 1)
                for y in span(dy, cells_y, 0, cells_y + 1)
            ]

        start_halo(STEPS + step, taken)
        if last:
            gather_in(part_a, got_a, share_a, out_a, 0)
        inner_cells(partial(backward_cell, step))
        if last:
            sums = acc_geo[...]
            tail = [sums[3 * f : 3 * f + 1] + sums[3 * f + 1 : 3 * f + 2] for f in range(3)]
            tail += [acc_small[0:1], jnp.zeros((4, width), F32)]
            few[0] = jnp.concatenate(tail, axis=0)
            sum_few_start(0, "gy", ngy, gy, few_y)
        d_recv = g_recv[...].reshape(cells * slots, width)
        put(4, outer(hs[step], d_recv))
        d_h = flow32 + rounded(mm_t(d_hid, w_nh[...])) + rounded(mm_t(d_recv, w_recv[...]))
        end_halo(STEPS + step)
        for d, (dx, dy) in enumerate(SIDES):
            at, rows_d = segs[d]
            arrived = halo_recv[STEPS + step, pl.ds(at, rows_d)].astype(F32)
            where = [
                (x, y)
                for x in span(dx, cells_x, cells_x, 1)
                for y in span(dy, cells_y, cells_y, 1)
            ]
            for i, (x, y) in enumerate(where):
                gext[x, y] += arrived[i * slots : (i + 1) * slots]
        d_send = jnp.concatenate(
            [
                gext[x + 1, pl.ds(1, cells_y)].reshape(cells_y * slots, width)
                for x in range(cells_x)
            ],
            axis=0,
        ).astype(BF16)
        put(5, outer(hs[step], d_send))
        if last:
            if part_b.shape[0] > 2 * width:
                part_b[pl.ds(2 * width, part_b.shape[0] - 2 * width)] = jnp.zeros(
                    (part_b.shape[0] - 2 * width, width), BF16
                )
            spread_out(part_b, got_b, share_b, 2)
            sum_few_end(0, few_y)
            sum_few_start(1, "gx", ngx, gx, few_x)
        flow = (d_h + rounded(mm_t(d_send, w_send[...]))).astype(BF16)
    grad_latent[...] = flow
    gather_in(part_b, got_b, share_b, out_b, 2)
    sum_few_end(1, few_x)
    out_few[...] = few[2]
    gathered(share_a, out_a, 0)
    gathered(share_b, out_b, 2)


def per_device(
    ngx,
    ngy,
    latent,
    positions,
    counts,
    cotangent,
    w_recv,
    w_send,
    w_msg,
    w_node_h,
    w_node_m,
    w_out,
    geometry,
    gain,
):
    cells_x, cells_y, slots, width = latent.shape
    cells = cells_x * cells_y
    rows = cells * slots
    n = ngx * ngy
    slot_index = lax.broadcasted_iota(jnp.int32, (cells_x, cells_y, slots), 2)
    validity = (slot_index < counts[:, :, None]).astype(F32)
    by_cell = jnp.concatenate(
        [
            positions[..., 0].astype(F32),
            positions[..., 1].astype(F32),
            validity,
            jnp.zeros((cells_x, cells_y, 128 - 3 * slots), F32),
        ],
        axis=-1,
    )
    pairs = 9 * slots * slots
    wide = -(-pairs // 128) * 128
    _, halo_rows = segments(cells_x, cells_y, slots)
    share_a = round16(-(-4 * width // n))
    share_b = round16(-(-2 * width // n))
    vmem = pltpu.VMEM
    scratch = [
        vmem((STEPS, cells_x + 2, cells_y + 2, slots, width), F32),
        vmem((cells_x + 2, cells_y + 2, slots, width), F32),
        vmem((STEPS, cells, slots, width), F32),
        vmem((cells, slots, width), F32),
        vmem((cells, slots, width), F32),
        vmem((cells, slots, width), F32),
        vmem((STEPS, rows, width), BF16),
        vmem((STEPS, rows, width), BF16),
        vmem((STEPS, rows, width), BF16),
        vmem((STEPS, rows, width), BF16),
        vmem((STEPS, rows, width), F32),
        vmem((STEPS, rows, width), F32),
        vmem((STEPS, rows, 128), F32),
        vmem((6, width, width), F32),
        vmem((8, width), F32),
        vmem((16, width), F32),
        vmem((8, cells_y, 128), F32),
        vmem((8, cells_y, 128), F32),
        vmem((cells_x + 2, -(-(cells_y + 2) // 8) * 8, 128), F32),
        vmem((3, cells, 128), F32),
        vmem((4, cells, wide), F32),
        vmem((cells, pairs, DEPTH), BF16),
        vmem((cells, DEPTH, pairs), BF16),
        vmem((DEPTH - GEO_AT, width), F32),
        vmem((2 * STEPS, halo_rows, width), BF16),
        vmem((2 * STEPS, halo_rows, width), BF16),
        vmem((n * share_a, width), BF16),
        vmem((n * share_b, width), BF16),
        vmem((n - 1, share_a, width), BF16),
        vmem((n - 1, share_b, width), BF16),
        vmem((3, 8, width), F32),
        vmem((ngy - 1, 8, width), F32),
        vmem((ngx - 1, 8, width), F32),
        pltpu.SemaphoreType.DMA((2,)),
        pltpu.SemaphoreType.DMA((2, 2 * STEPS)),
        pltpu.SemaphoreType.DMA((2, 4)),
        pltpu.SemaphoreType.DMA((2, 2)),
    ]
    spec = pl.BlockSpec(memory_space=pltpu.VMEM)
    new, flow, sums_a, sums_b, sums_few = pl.pallas_call(
        partial(kernel, ngx, ngy, cells_x, cells_y),
        out_shape=[
            jax.ShapeDtypeStruct((rows, width), BF16),
            jax.ShapeDtypeStruct((rows, width), BF16),
            jax.ShapeDtypeStruct((n * share_a, width), BF16),
            jax.ShapeDtypeStruct((n * share_b, width), BF16),
            jax.ShapeDtypeStruct((8, width), F32),
        ],
        in_specs=[spec] * 11,
        out_specs=[spec] * 5,
        scratch_shapes=scratch,
        compiler_params=pltpu.CompilerParams(
            collective_id=0, has_side_effects=True, vmem_limit_bytes=56 * 2**20
        ),
        name="evolver",
    )(
        latent.reshape(rows, width),
        by_cell,
        cotangent.reshape(rows, width),
        w_recv,
        w_send,
        w_msg,
        w_node_h,
        w_node_m,
        w_out,
        geometry,
        gain.reshape(1, width),
    )

    def piece(sums, at, size):
        return sums[at : at + size].astype(F32)

    return (
        new.reshape(latent.shape),
        flow.reshape(latent.shape),
        piece(sums_b, 0, width),
        piece(sums_b, width, width),
        piece(sums_a, 0, width),
        piece(sums_a, width, width),
        piece(sums_a, 2 * width, width),
        piece(sums_a, 3 * width, width),
        sums_few[:3],
        sums_few[3],
    )


def solution(mesh):
    cell_spec = P(("groups", "gx"), "gy", None, None)
    placed = (cell_spec, cell_spec, P(("groups", "gx"), "gy"), cell_spec) + (P(),) * 8
    return jax.shard_map(
        partial(per_device, mesh.shape["gx"], mesh.shape["gy"]),
        mesh=mesh,
        in_specs=placed,
        out_specs=(cell_spec, cell_spec) + (P("groups", None),) * 7 + (P("groups"),),
        check_vma=False,
    )
```
